32 devices in a mesh: lon: 4 (over y, x), lat: 4 (over z), phys: 2 (over core).
Axes of the slice: x: 2, y: 2, z: 4, core: 2. Of those that a mesh axis runs over, the one named last changes fastest.
Arguments:
- tracers: float32 [5, 128, 16, 1024], P(None, 'phys', 'lat', 'lon'), may hold values from -6 to 6
- wind_field: float32 [2, 128, 16, 1024], P(None, 'phys', 'lat', 'lon'), may hold values from -0.3 to 0.3
- diffusivity: float32 [128, 16, 1024], P('phys', 'lat', 'lon'), may hold values from 0.03 to 0.2
- weight_in: bfloat16 [256, 5, 128], replicated, may hold values from -0.25 to 0.25
- bias_in: float32 [256], replicated, may hold values from -3 to 3
- weight_mid: bfloat16 [256, 256], replicated, may hold values from -0.375 to 0.375
- bias_mid: float32 [256], replicated, may hold values from -3 to 3
- weight_out: bfloat16 [5, 128, 256], replicated, may hold values from -0.375 to 0.375
- bias_out: float32 [5, 128], replicated, may hold values from -2 to 2
Outputs:
- new_tracers: float32 [5, 128, 16, 1024], P(None, 'phys', 'lat', 'lon')
The draws below stay inside these ranges and needn't reach their ends.
All inputs are finite; a program needn't handle non-finite values.
Results may differ from the reference program's by a relative error of at most 0.0029.
Values may be sent and summed in bfloat16 or wider, within the bound.
A program may use at most 64 MiB of HBM per device.

```python
import math
import jax
import jax.numpy as jnp

F = 5
LEV = 128
HID = 256
NLAT = 16
NLON = 1024


def block_scale(stream_key, shape, cuts, least, top_value):
    gain, own = 1.0, jax.random.fold_in(stream_key, 6)
    for axis_at, blocks in cuts:
        draws = jnp.exp(jax.random.uniform(jax.random.fold_in(own, axis_at), (blocks,), jnp.float32, least / len(cuts), top_value / len(cuts)))
        gain = gain * jnp.repeat(draws, shape[axis_at] // blocks).reshape([-1 if axis == axis_at else 1 for axis in range(len(shape))])
    return gain


def gaussian(key, dims, spread, most, split=(), kind=jnp.bfloat16):
    gain = block_scale(key, dims, split, -0.22, 0.18) if split else 1.0
    drawn = jax.random.normal(key, dims, jnp.float32) * spread * gain
    return jnp.minimum(jnp.maximum(drawn, -most), most).astype(kind)


def setup_inputs(seed: int = 0) -> dict:
    key_list = jax.random.split(jax.random.key(seed), 10)
    tracers = gaussian(key_list[0], (F, LEV, NLAT, NLON), 1.0, 6.0, ((1, 2), (2, 4), (3, 4)), jnp.float32)
    wind_field = jnp.clip(jax.random.uniform(key_list[1], (2, LEV, NLAT, NLON), jnp.float32, -0.3, 0.3) * block_scale(key_list[1], (2, LEV, NLAT, NLON), ((1, 2), (2, 4), (3, 4)), -0.4, 0.0), -0.3, 0.3)
    diffusivity = jnp.clip(jnp.exp(math.log(0.2) - 1.89712 * jax.random.uniform(key_list[2], (LEV, NLAT, NLON), jnp.float32) ** block_scale(key_list[2], (LEV, NLAT, NLON), ((0, 2), (1, 4), (2, 4)), -0.2, 0.2)), 0.03, 0.2)
    weight_in = gaussian(key_list[3], (HID, F, LEV), (F * LEV) ** -0.5, 0.25)
    bias_in = gaussian(key_list[4], (HID,), 0.5, 3.0, (), jnp.float32)
    weight_mid = gaussian(key_list[5], (HID, HID), HID ** -0.5, 0.375)
    bias_mid = gaussian(key_list[6], (HID,), 0.5, 3.0, (), jnp.float32)
    weight_out = gaussian(key_list[7], (F, LEV, HID), HID ** -0.5, 0.375)
    bias_out = gaussian(key_list[8], (F, LEV), 0.3, 2.0, (), jnp.float32)
    return dict(tracers=tracers, wind_field=wind_field, diffusivity=diffusivity, weight_in=weight_in, bias_in=bias_in, weight_mid=weight_mid, bias_mid=bias_mid, weight_out=weight_out, bias_out=bias_out)


def advance(center, eastward, westward, northward, southward, wind_east, wind_north, diffuse):
    return (center - 0.5 * wind_east * (eastward - westward) - 0.5 * wind_north * (northward - southward)
            + diffuse * (eastward + westward + northward + southward - 4.0 * center))


def substep(field, wind_field, diffusivity):
    eastward = jnp.roll(field, -1, axis=3)
    westward = jnp.roll(field, 1, axis=3)
    zero_row = jnp.zeros_like(field[:, :, :1])
    northward = jnp.concatenate([field[:, :, 1:], zero_row], axis=2)
    southward = jnp.concatenate([zero_row, field[:, :, :-1]], axis=2)
    return advance(field, eastward, westward, northward, southward, wind_field[0], wind_field[1], diffusivity)


def reference(tracers, wind_field, diffusivity, weight_in, bias_in, weight_mid, bias_mid, weight_out, bias_out):
    field = tracers
    for substep_index in range(2):
        field = substep(field, wind_field, diffusivity)
    column_input = field.astype(jnp.bfloat16).reshape(F * LEV, NLAT * NLON)
    pre_first = jnp.dot(weight_in.reshape(HID, F * LEV), column_input, preferred_element_type=jnp.float32) + bias_in[:, None]
    act_first = jax.nn.silu(pre_first).astype(jnp.bfloat16)
    pre_second = jnp.dot(weight_mid, act_first, preferred_element_type=jnp.float32) + bias_mid[:, None]
    act_second = jax.nn.silu(pre_second).astype(jnp.bfloat16)
    projected = jnp.dot(weight_out.reshape(F * LEV, HID), act_second, preferred_element_type=jnp.float32)
    tendency = (projected + bias_out.reshape(F * LEV)[:, None]).astype(jnp.bfloat16)
    return field + tendency.astype(jnp.float32).reshape(field.shape)
```

```python
import functools

import jax
import jax.numpy as jnp
from jax import lax
from jax.experimental import pallas as pl
from jax.experimental.pallas import tpu as pltpu
from jax.sharding import PartitionSpec as P

LANES = 128
BLK = 16
MESH = pl.DeviceIdType.MESH
f32, bf16 = jnp.float32, jnp.bfloat16


def silu(z):
    half = 0.5 * z
    return half + half * jnp.tanh(half)


def kernel(
    dims, tr_hbm, wind_hbm, diff_hbm, w1_hbm, b1_hbm, w2_hbm, b2_hbm, w3_hbm, b3_hbm, out_hbm,
    raw, wraw, draw, w1, w2, w3, b1r, b2r, b3r, b1, b2, b3,
    q0, q1, adv, cf, zs, zr, ls, lr, xb, oraw,
    in_sem, out_sem, zs_sem, zr_sem, ls_sem, lr_sem, xs_sem, xr_sem,
):
    F, L, R, C, H, LEV = dims
    tiles = C // LANES
    step_rows = tiles * R
    lon, lat, phys = (lax.axis_index(a) for a in ("lon", "lat", "phys"))
    nlon, nlat = lax.axis_size("lon"), lax.axis_size("lat")
    east, west = lax.rem(lon + 1, nlon), lax.rem(lon + nlon - 1, nlon)
    north, south = jnp.minimum(lat + 1, nlat - 1), jnp.maximum(lat - 1, 0)
    has_north, has_south = lat < nlat - 1, lat > 0
    other = 1 - phys
    own = pl.multiple_of(phys * L, L)

    loads = [pltpu.make_async_copy(
        tr_hbm.at[pl.ds(f * L * step_rows, L * step_rows)],
        raw.at[pl.ds(f * L * step_rows, L * step_rows)], in_sem.at[f]) for f in range(F)]
    pairs = [(wind_hbm, wraw), (diff_hbm, draw), (b1_hbm, b1r), (b2_hbm, b2r), (b3_hbm, b3r), (w2_hbm, w2)]
    pairs += [(w1_hbm.at[f], w1.at[:, pl.ds(f * LEV, LEV)]) for f in range(F)]
    pairs += [(w3_hbm.at[f, pl.ds(own, L)], w3.at[pl.ds(f * L, L)]) for f in range(F)]
    loads += [pltpu.make_async_copy(s, d, in_sem.at[F + k]) for k, (s, d) in enumerate(pairs)]
    for copy in loads:
        copy.start()

    barrier = pltpu.get_barrier_semaphore()
    for d in ({"lon": east}, {"lon": west}, {"phys": other}):
        pl.semaphore_signal(barrier, inc=1, device_id=d, device_id_type=MESH)

    @pl.when(has_north)
    def _():
        pl.semaphore_signal(barrier, inc=1, device_id={"lat": north}, device_id_type=MESH)

    @pl.when(has_south)
    def _():
        pl.semaphore_signal(barrier, inc=1, device_id={"lat": south}, device_id_type=MESH)

    def lat_copy(rnd, side, f):
        return pltpu.make_async_remote_copy(
            src_ref=zs.at[rnd, side, f], dst_ref=zr.at[rnd, side, f],
            send_sem=zs_sem.at[rnd, side, f], recv_sem=zr_sem.at[rnd, side, f],
            device_id={"lat": south if side else north}, device_id_type=MESH)

    def lon_copy(m, side):
        return pltpu.make_async_remote_copy(
            src_ref=ls.at[m, side], dst_ref=lr.at[m, side],
            send_sem=ls_sem.at[m, side], recv_sem=lr_sem.at[m, side],
            device_id={"lon": west if side else east}, device_id_type=MESH)

    def x_copy(ph, f):
        rows = pl.ds(pl.multiple_of(f * LEV + phys * L, L), L)
        return pltpu.make_async_remote_copy(
            src_ref=xb.at[ph, :, rows], dst_ref=xb.at[ph, :, rows],
            send_sem=xs_sem.at[ph, f], recv_sem=xr_sem.at[ph, f],
            device_id={"phys": other}, device_id_type=MESH)

    can_send = (has_north, has_south)
    can_recv = (has_south, has_north)

    def lat_start(rnd, f):
        for side in range(2):
            @pl.when(can_send[side])
            def _():
                lat_copy(rnd, side, f).start()

    def lat_wait(rnd, f):
        for side in range(2):
            @pl.when(can_recv[side])
            def _():
                lat_copy(rnd, side, f).wait_recv()

    for side, there in enumerate(can_recv):
        @pl.when(jnp.logical_not(there))
        def _():
            zr[:, side] = jnp.zeros(zr.shape[:1] + zr.shape[2:], bf16)

    lane = lax.broadcasted_iota(jnp.int32, (BLK, LANES), 1)
    wide = lax.broadcasted_iota(jnp.int32, (BLK, C), 1)

    def blocks(body):
        def run(k, carry):
            body(pl.ds(pl.multiple_of(k * BLK, BLK), BLK), k * BLK)
            return carry
        lax.fori_loop(0, L // BLK, run, 0)

    def spaced(f, r, level, t):
        return pl.ds(((f * L + level) * tiles + t) * R + r, BLK, stride=step_rows)

    def natural(ref, f, r, level):
        return jnp.concatenate([ref[spaced(f, r, level, t), :] for t in range(tiles)], axis=1)

    def pack(q, rows, m):
        def body(lev, _):
            to_east = jnp.zeros((BLK, LANES), f32)
            to_west = jnp.zeros((BLK, LANES), f32)
            for f in range(F):
                for r in rows:
                    j = f * R + r
                    last = q[f, r, lev, C - LANES:]
                    first = q[f, r, lev, :LANES]
                    to_east = jnp.where(lane == j, jnp.broadcast_to(last[:, LANES - 1:], (BLK, LANES)), to_east)
                    to_west = jnp.where(lane == j, jnp.broadcast_to(first[:, :1], (BLK, LANES)), to_west)
            ls[m, 0, lev, :] = to_east.astype(bf16)
            ls[m, 1, lev, :] = to_west.astype(bf16)
        blocks(body)
        for side in range(2):
            lon_copy(m, side).start()

    def stencil(q, f, r, lev, rnd, m):
        j = f * R + r
        c = q[f, r, lev, :]
        hw = lr[m, 0, lev, :].astype(f32)[:, j:j + 1]
        he = lr[m, 1, lev, :].astype(f32)[:, j:j + 1]
        w = jnp.where(wide == 0, jnp.broadcast_to(hw, (BLK, C)), pltpu.roll(c, 1, 1))
        e = jnp.where(wide == C - 1, jnp.broadcast_to(he, (BLK, C)), pltpu.roll(c, C - 1, 1))
        s = q[f, r - 1, lev, :] if r else zr[rnd, 0, f, lev, :].astype(f32)
        n = q[f, r + 1, lev, :] if r < R - 1 else zr[rnd, 1, f, lev, :].astype(f32)
        return (cf[0, r, lev, :] * c + cf[1, r, lev, :] * e + cf[2, r, lev, :] * w
                + cf[3, r, lev, :] * n + cf[4, r, lev, :] * s)

    edge, inner = (0, R - 1), tuple(range(1, R - 1))
    phases = (inner, edge)

    for f in range(F):
        loads[f].wait()

        def body(lev, level):
            for r in range(R):
                v = natural(raw, f, r, level)
                q0[f, r, lev, :] = v
                if r == R - 1:
                    zs[0, 0, f, lev, :] = v.astype(bf16)
                if r == 0:
                    zs[0, 1, f, lev, :] = v.astype(bf16)
        blocks(body)

    pl.semaphore_wait(barrier, 3 + has_north.astype(jnp.int32) + has_south.astype(jnp.int32))
    for f in range(F):
        lat_start(0, f)
    pack(q0, range(R), 0)

    for copy in loads[F:]:
        copy.wait()

    def coefficients(lev, level):
        for r in range(R):
            u = 0.5 * natural(wraw, 0, r, level)
            v = 0.5 * natural(wraw, 1, r, level)
            nu = natural(draw, 0, r, level)
            cf[0, r, lev, :] = 1.0 - 4.0 * nu
            cf[1, r, lev, :] = nu - u
            cf[2, r, lev, :] = nu + u
            cf[3, r, lev, :] = nu - v
            cf[4, r, lev, :] = nu + v
    blocks(coefficients)

    def columns(row):
        return jnp.transpose(jnp.broadcast_to(row, (LANES, LANES)))

    for k in range(H // LANES):
        b1[k * LANES:(k + 1) * LANES, :] = columns(b1r[k:k + 1, :])
        b2[k * LANES:(k + 1) * LANES, :] = columns(b2r[k:k + 1, :])
    for f in range(F):
        b3[f] = columns(b3r[f:f + 1, :])

    for side in range(2):
        lon_copy(0, side).wait_recv()

    def first_inner(lev, level):
        for r in inner:
            for f in range(F):
                q1[f, r, lev, :] = stencil(q0, f, r, lev, 0, 0)
    blocks(first_inner)
    pack(q1, inner, 1)

    for f in range(F):
        lat_wait(0, f)

        def first_edge(lev, level):
            for side, r in ((1, 0), (0, R - 1)):
                v = stencil(q0, f, r, lev, 0, 0)
                q1[f, r, lev, :] = v
                zs[1, side, f, lev, :] = v.astype(bf16)
        blocks(first_edge)
        lat_start(1, f)
    pack(q1, edge, 2)

    def second(f, ph, m):
        def body(lev, level):
            for i, r in enumerate(phases[ph]):
                v = stencil(q1, f, r, lev, 1, m)
                adv[ph, i, f, lev, :] = v
                xb[ph, i, pl.ds(pl.multiple_of(f * LEV + phys * L + level, BLK), BLK), :] = v.astype(bf16)
        blocks(body)
        x_copy(ph, f).start()

    def bias(ref):
        return jnp.concatenate([ref] * tiles, axis=1)

    def physics(ph):
        for i, r in enumerate(phases[ph]):
            pre = jnp.dot(w1[...], xb[ph, i], preferred_element_type=f32)
            act = silu(pre + bias(b1[...])).astype(bf16)
            pre = jnp.dot(w2[...], act, preferred_element_type=f32)
            act = silu(pre + bias(b2[...])).astype(bf16)
            for f in range(F):
                proj = jnp.dot(w3[f * L:(f + 1) * L, :], act, preferred_element_type=f32)
                ten = (proj + bias(b3[f, pl.ds(own, L), :])).astype(bf16).astype(f32)
                res = adv[ph, i, f] + ten
                for t in range(tiles):
                    oraw[pl.ds((f * L * tiles + t) * R + r, L, stride=step_rows), :] = (
                        res[:, t * LANES:(t + 1) * LANES])

    for side in range(2):
        lon_copy(1, side).wait_recv()
    for f in range(F):
        second(f, 0, 1)
    for f in range(F):
        x_copy(0, f).wait_recv()
    physics(0)

    for side in range(2):
        lon_copy(2, side).wait_recv()
    for f in range(F):
        lat_wait(1, f)
        second(f, 1, 2)
    for f in range(F):
        x_copy(1, f).wait_recv()
    physics(1)

    out = pltpu.make_async_copy(oraw, out_hbm, out_sem)
    out.start()
    for f in range(F):
        for rnd in range(2):
            for side in range(2):
                @pl.when(can_send[side])
                def _():
                    lat_copy(rnd, side, f).wait_send()
            x_copy(rnd, f).wait_send()
    for m in range(3):
        for side in range(2):
            lon_copy(m, side).wait_send()
    out.wait()


def as_stored(a, tiles):
    lead, rows = a.shape[:-2], a.shape[-2]
    a = a.reshape(lead + (rows, tiles, LANES))
    return jnp.swapaxes(a, -3, -2).reshape(-1, LANES)


def shards(tracers, wind_field, diffusivity, weight_in, bias_in, weight_mid, bias_mid, weight_out, bias_out):
    F, L, R, C = tracers.shape
    H, _, LEV = weight_in.shape
    tiles = C // LANES
    n = tracers.size // LANES
    dma = pltpu.SemaphoreType.DMA
    V = pltpu.VMEM
    out = pl.pallas_call(
        functools.partial(kernel, (F, L, R, C, H, LEV)),
        out_shape=jax.ShapeDtypeStruct((n, LANES), f32),
        in_specs=[pl.BlockSpec(memory_space=pl.ANY)] * 9,
        out_specs=pl.BlockSpec(memory_space=pl.ANY),
        scratch_shapes=[
            V((n, LANES), f32), V((2 * n // F, LANES), f32), V((n // F, LANES), f32),
            V((H, F * LEV), bf16), V((H, H), bf16), V((F * L, H), bf16),
            V((H // LANES, LANES), f32), V((H // LANES, LANES), f32), V((F, LEV), f32),
            V((H, LANES), f32), V((H, LANES), f32), V((F, LEV, LANES), f32),
            V((F, R, L, C), f32), V((F, R, L, C), f32), V((2, 2, F, L, C), f32), V((5, R, L, C), f32),
            V((2, 2, F, L, C), bf16), V((2, 2, F, L, C), bf16),
            V((3, 2, L, LANES), bf16), V((3, 2, L, LANES), bf16),
            V((2, 2, F * LEV, C), bf16), V((n, LANES), f32),
            dma((3 * F + 6,)), dma, dma((2, 2, F)), dma((2, 2, F)), dma((3, 2)), dma((3, 2)),
            dma((2, F)), dma((2, F)),
        ],
        compiler_params=pltpu.CompilerParams(
            collective_id=0, has_side_effects=True, vmem_limit_bytes=40 * 2**20),
    )(
        as_stored(tracers, tiles), as_stored(wind_field, tiles), as_stored(diffusivity, tiles),
        jnp.swapaxes(weight_in, 0, 1), bias_in.reshape(-1, LANES), weight_mid,
        bias_mid.reshape(-1, LANES), weight_out, bias_out,
    )
    out = out.reshape(F, L, tiles, R, LANES)
    return jnp.swapaxes(out, 2, 3).reshape(F, L, R, C)


def solution(mesh):
    placed = (
        P(None, "phys", "lat", "lon"), P(None, "phys", "lat", "lon"), P("phys", "lat", "lon"),
        P(), P(), P(), P(), P(), P(),
    )
    return jax.shard_map(
        shards, mesh=mesh, in_specs=placed, out_specs=P(None, "phys", "lat", "lon"), check_vma=False
    )
```

```python
import functools

import jax
import jax.numpy as jnp
from jax import lax
from jax.experimental import pallas as pl
from jax.experimental.pallas import tpu as pltpu
from jax.sharding import PartitionSpec as P

LANES = 128
BLK = 16
MESH = pl.DeviceIdType.MESH
f32, bf16 = jnp.float32, jnp.bfloat16


def silu(z):
    half = 0.5 * z
    return half + half * jnp.tanh(half)


def kernel(
    dims, tr_hbm, wind_hbm, diff_hbm, w1_hbm, b1_hbm, w2_hbm, b2_hbm, w3_hbm, b3_hbm, oraw,
    raw, wraw, draw, w1, w2, w3, b1r, b2r, b3r, b1, b2, b3,
    q0, q1, adv, cf, zs, zr, ls, lr, xb,
    in_sem, zs_sem, zr_sem, ls_sem, lr_sem, xs_sem, xr_sem,
):
    F, L, R, C, H, LEV = dims
    tiles = C // LANES
    step_rows = tiles * R
    lon, lat, phys = (lax.axis_index(a) for a in ("lon", "lat", "phys"))
    nlon, nlat = lax.axis_size("lon"), lax.axis_size("lat")
    east, west = lax.rem(lon + 1, nlon), lax.rem(lon + nlon - 1, nlon)
    north, south = jnp.minimum(lat + 1, nlat - 1), jnp.maximum(lat - 1, 0)
    has_north, has_south = lat < nlat - 1, lat > 0
    other = 1 - phys
    own = pl.multiple_of(phys * L, L)

    loads = [pltpu.make_async_copy(
        tr_hbm.at[pl.ds(f * L * step_rows, L * step_rows)],
        raw.at[pl.ds(f * L * step_rows, L * step_rows)], in_sem.at[f]) for f in range(F)]
    pairs = [(wind_hbm, wraw), (diff_hbm, draw), (b1_hbm, b1r), (b2_hbm, b2r), (b3_hbm, b3r), (w2_hbm, w2)]
    pairs += [(w1_hbm.at[f], w1.at[:, pl.ds(f * LEV, LEV)]) for f in range(F)]
    pairs += [(w3_hbm.at[f, pl.ds(own, L)], w3.at[pl.ds(f * L, L)]) for f in range(F)]
    loads += [pltpu.make_async_copy(s, d, in_sem.at[F + k]) for k, (s, d) in enumerate(pairs)]
    for copy in loads:
        copy.start()

    barrier = pltpu.get_barrier_semaphore()
    for d in ({"lon": east}, {"lon": west}, {"phys": other}):
        pl.semaphore_signal(barrier, inc=1, device_id=d, device_id_type=MESH)

    @pl.when(has_north)
    def _():
        pl.semaphore_signal(barrier, inc=1, device_id={"lat": north}, device_id_type=MESH)

    @pl.when(has_south)
    def _():
        pl.semaphore_signal(barrier, inc=1, device_id={"lat": south}, device_id_type=MESH)

    def lat_copy(rnd, side, f):
        return pltpu.make_async_remote_copy(
            src_ref=zs.at[rnd, side, f], dst_ref=zr.at[rnd, side, f],
            send_sem=zs_sem.at[rnd, side, f], recv_sem=zr_sem.at[rnd, side, f],
            device_id={"lat": south if side else north}, device_id_type=MESH)

    def lon_copy(m, side):
        return pltpu.make_async_remote_copy(
            src_ref=ls.at[m, side], dst_ref=lr.at[m, side],
            send_sem=ls_sem.at[m, side], recv_sem=lr_sem.at[m, side],
            device_id={"lon": west if side else east}, device_id_type=MESH)

    def x_copy(ph, f):
        rows = pl.ds(pl.multiple_of(f * LEV + phys * L, L), L)
        return pltpu.make_async_remote_copy(
            src_ref=xb.at[ph, :, rows], dst_ref=xb.at[ph, :, rows],
            send_sem=xs_sem.at[ph, f], recv_sem=xr_sem.at[ph, f],
            device_id={"phys": other}, device_id_type=MESH)

    can_send = (has_north, has_south)
    can_recv = (has_south, has_north)

    def lat_start(rnd, f):
        for side in range(2):
            @pl.when(can_send[side])
            def _():
                lat_copy(rnd, side, f).start()

    def lat_wait(rnd, f):
        for side in range(2):
            @pl.when(can_recv[side])
            def _():
                lat_copy(rnd, side, f).wait_recv()

    for side, there in enumerate(can_recv):
        @pl.when(jnp.logical_not(there))
        def _():
            zr[:, side] = jnp.zeros(zr.shape[:1] + zr.shape[2:], bf16)

    lane = lax.broadcasted_iota(jnp.int32, (BLK, LANES), 1)
    wide = lax.broadcasted_iota(jnp.int32, (BLK, C), 1)

    def blocks(body):
        def run(k, carry):
            body(pl.ds(pl.multiple_of(k * BLK, BLK), BLK), k * BLK)
            return carry
        lax.fori_loop(0, L // BLK, run, 0, unroll=True)

    def spaced(f, r, level, t):
        return pl.ds(((f * L + level) * tiles + t) * R + r, BLK, stride=step_rows)

    def natural(ref, f, r, level):
        return jnp.concatenate([ref[spaced(f, r, level, t), :] for t in range(tiles)], axis=1)

    def pack(q, rows, m):
        def body(lev, _):
            to_east = jnp.zeros((BLK, LANES), f32)
            to_west = jnp.zeros((BLK, LANES), f32)
            for f in range(F):
                for r in rows:
                    j = f * R + r
                    last = q[f, r, lev, C - LANES:]
                    first = q[f, r, lev, :LANES]
                    to_east = jnp.where(lane == j, jnp.broadcast_to(last[:, LANES - 1:], (BLK, LANES)), to_east)
                    to_west = jnp.where(lane == j, jnp.broadcast_to(first[:, :1], (BLK, LANES)), to_west)
            ls[m, 0, lev, :] = to_east.astype(bf16)
            ls[m, 1, lev, :] = to_west.astype(bf16)
        blocks(body)
        for side in range(2):
            lon_copy(m, side).start()

    def stencil(q, f, r, lev, rnd, m):
        j = f * R + r
        c = q[f, r, lev, :]
        hw = lr[m, 0, lev, :].astype(f32)[:, j:j + 1]
        he = lr[m, 1, lev, :].astype(f32)[:, j:j + 1]
        w = jnp.where(wide == 0, jnp.broadcast_to(hw, (BLK, C)), pltpu.roll(c, 1, 1))
        e = jnp.where(wide == C - 1, jnp.broadcast_to(he, (BLK, C)), pltpu.roll(c, C - 1, 1))
        s = q[f, r - 1, lev, :] if r else zr[rnd, 0, f, lev, :].astype(f32)
        n = q[f, r + 1, lev, :] if r < R - 1 else zr[rnd, 1, f, lev, :].astype(f32)
        return (cf[0, r, lev, :] * c + cf[1, r, lev, :] * e + cf[2, r, lev, :] * w
                + cf[3, r, lev, :] * n + cf[4, r, lev, :] * s)

    edge, inner = (0, R - 1), tuple(range(1, R - 1))
    phases = (inner, edge)

    for f in range(F):
        loads[f].wait()

        def body(lev, level):
            for r in range(R):
                v = natural(raw, f, r, level)
                q0[f, r, lev, :] = v
                if r == R - 1:
                    zs[0, 0, f, lev, :] = v.astype(bf16)
                if r == 0:
                    zs[0, 1, f, lev, :] = v.astype(bf16)
        blocks(body)

    pl.semaphore_wait(barrier, 3 + has_north.astype(jnp.int32) + has_south.astype(jnp.int32))
    for f in range(F):
        lat_start(0, f)
    pack(q0, range(R), 0)

    for copy in loads[F:]:
        copy.wait()

    def coefficients(lev, level):
        for r in range(R):
            u = 0.5 * natural(wraw, 0, r, level)
            v = 0.5 * natural(wraw, 1, r, level)
            nu = natural(draw, 0, r, level)
            cf[0, r, lev, :] = 1.0 - 4.0 * nu
            cf[1, r, lev, :] = nu - u
            cf[2, r, lev, :] = nu + u
            cf[3, r, lev, :] = nu - v
            cf[4, r, lev, :] = nu + v
    blocks(coefficients)

    def columns(row):
        return jnp.transpose(jnp.broadcast_to(row, (LANES, LANES)))

    for k in range(H // LANES):
        b1[k * LANES:(k + 1) * LANES, :] = columns(b1r[k:k + 1, :])
        b2[k * LANES:(k + 1) * LANES, :] = columns(b2r[k:k + 1, :])
    for f in range(F):
        b3[f] = columns(b3r[f:f + 1, :])

    for side in range(2):
        lon_copy(0, side).wait_recv()

    def first_inner(lev, level):
        for r in inner:
            for f in range(F):
                q1[f, r, lev, :] = stencil(q0, f, r, lev, 0, 0)
    blocks(first_inner)
    pack(q1, inner, 1)

    for f in range(F):
        lat_wait(0, f)

        def first_edge(lev, level):
            for side, r in ((1, 0), (0, R - 1)):
                v = stencil(q0, f, r, lev, 0, 0)
                q1[f, r, lev, :] = v
                zs[1, side, f, lev, :] = v.astype(bf16)
        blocks(first_edge)
        lat_start(1, f)
    pack(q1, edge, 2)

    def second(f, ph, m):
        def body(lev, level):
            for i, r in enumerate(phases[ph]):
                v = stencil(q1, f, r, lev, 1, m)
                adv[ph, i, f, lev, :] = v
                xb[ph, i, pl.ds(pl.multiple_of(f * LEV + phys * L + level, BLK), BLK), :] = v.astype(bf16)
        blocks(body)
        x_copy(ph, f).start()

    def bias(ref):
        return jnp.concatenate([ref] * tiles, axis=1)

    def physics(ph):
        for i, r in enumerate(phases[ph]):
            pre = jnp.dot(w1[...], xb[ph, i], preferred_element_type=f32)
            act = silu(pre + bias(b1[...])).astype(bf16)
            pre = jnp.dot(w2[...], act, preferred_element_type=f32)
            act = silu(pre + bias(b2[...])).astype(bf16)
            for f in range(F):
                proj = jnp.dot(w3[f * L:(f + 1) * L, :], act, preferred_element_type=f32)
                ten = (proj + bias(b3[f, pl.ds(own, L), :])).astype(bf16).astype(f32)
                res = adv[ph, i, f] + ten
                for t in range(tiles):
                    oraw[pl.ds((f * L * tiles + t) * R + r, L, stride=step_rows), :] = (
                        res[:, t * LANES:(t + 1) * LANES])

    for side in range(2):
        lon_copy(1, side).wait_recv()
    for f in range(F):
        second(f, 0, 1)
    for f in range(F):
        x_copy(0, f).wait_recv()
    physics(0)

    for side in range(2):
        lon_copy(2, side).wait_recv()
    for f in range(F):
        lat_wait(1, f)
        second(f, 1, 2)
    for f in range(F):
        x_copy(1, f).wait_recv()
    physics(1)

    for f in range(F):
        for rnd in range(2):
            for side in range(2):
                @pl.when(can_send[side])
                def _():
                    lat_copy(rnd, side, f).wait_send()
            x_copy(rnd, f).wait_send()
    for m in range(3):
        for side in range(2):
            lon_copy(m, side).wait_send()


def as_stored(a, tiles):
    lead, rows = a.shape[:-2], a.shape[-2]
    a = a.reshape(lead + (rows, tiles, LANES))
    return jnp.swapaxes(a, -3, -2).reshape(-1, LANES)


def shards(tracers, wind_field, diffusivity, weight_in, bias_in, weight_mid, bias_mid, weight_out, bias_out):
    F, L, R, C = tracers.shape
    H, _, LEV = weight_in.shape
    tiles = C // LANES
    n = tracers.size // LANES
    dma = pltpu.SemaphoreType.DMA
    V = pltpu.VMEM
    out = pl.pallas_call(
        functools.partial(kernel, (F, L, R, C, H, LEV)),
        out_shape=jax.ShapeDtypeStruct((n, LANES), f32),
        in_specs=[pl.BlockSpec(memory_space=pltpu.HBM)] * 9,
        out_specs=pl.BlockSpec(memory_space=pltpu.VMEM),
        scratch_shapes=[
            V((n, LANES), f32), V((2 * n // F, LANES), f32), V((n // F, LANES), f32),
            V((H, F * LEV), bf16), V((H, H), bf16), V((F * L, H), bf16),
            V((H // LANES, LANES), f32), V((H // LANES, LANES), f32), V((F, LEV), f32),
            V((H, LANES), f32), V((H, LANES), f32), V((F, LEV, LANES), f32),
            V((F, R, L, C), f32), V((F, R, L, C), f32), V((2, 2, F, L, C), f32), V((5, R, L, C), f32),
            V((2, 2, F, L, C), bf16), V((2, 2, F, L, C), bf16),
            V((3, 2, L, LANES), bf16), V((3, 2, L, LANES), bf16),
            V((2, 2, F * LEV, C), bf16),
            dma((3 * F + 6,)), dma((2, 2, F)), dma((2, 2, F)), dma((3, 2)), dma((3, 2)),
            dma((2, F)), dma((2, F)),
        ],
        compiler_params=pltpu.CompilerParams(
            collective_id=0, has_side_effects=True, vmem_limit_bytes=32 * 2**20),
    )(*(pltpu.with_memory_space_constraint(a, pltpu.HBM) for a in (
        as_stored(tracers, tiles), as_stored(wind_field, tiles), as_stored(diffusivity, tiles),
        jnp.swapaxes(weight_in, 0, 1), bias_in.reshape(-1, LANES), weight_mid,
        bias_mid.reshape(-1, LANES), weight_out, bias_out,
    )))
    out = out.reshape(F, L, tiles, R, LANES)
    return jnp.swapaxes(out, 2, 3).reshape(F, L, R, C)


def solution(mesh):
    placed = (
        P(None, "phys", "lat", "lon"), P(None, "phys", "lat", "lon"), P("phys", "lat", "lon"),
        P(), P(), P(), P(), P(), P(),
    )
    return jax.shard_map(
        shards, mesh=mesh, in_specs=placed, out_specs=P(None, "phys", "lat", "lon"), check_vma=False
    )
```

```python
import functools

import jax
import jax.numpy as jnp
from jax import lax
from jax.experimental import pallas as pl
from jax.experimental.pallas import tpu as pltpu
from jax.sharding import PartitionSpec as P

LANES = 128
BLK = 16
MESH = pl.DeviceIdType.MESH
f32, bf16 = jnp.float32, jnp.bfloat16


def silu(z):
    half = 0.5 * z
    return half + half * jnp.tanh(half)


def kernel(
    dims, tr_hbm, wind_hbm, diff_hbm, w1_hbm, b1_hbm, w2_hbm, b2_hbm, w3_hbm, b3_hbm, oraw,
    raw, wraw, draw, w1, w2, w3, b1r, b2r, b3r, b1, b2, b3,
    q0, q1, adv, cf, zs, zr, ls, lr, xb,
    in_sem, zs_sem, zr_sem, ls_sem, lr_sem, xs_sem, xr_sem,
):
    F, L, R, C, H, LEV = dims
    tiles = C // LANES
    step_rows = tiles * R
    lon, lat, phys = (lax.axis_index(a) for a in ("lon", "lat", "phys"))
    nlon, nlat = lax.axis_size("lon"), lax.axis_size("lat")
    east, west = lax.rem(lon + 1, nlon), lax.rem(lon + nlon - 1, nlon)
    north, south = jnp.minimum(lat + 1, nlat - 1), jnp.maximum(lat - 1, 0)
    has_north, has_south = lat < nlat - 1, lat > 0
    other = 1 - phys
    own = pl.multiple_of(phys * L, L)

    loads = [pltpu.make_async_copy(
        tr_hbm.at[pl.ds(f * L * step_rows, L * step_rows)],
        raw.at[pl.ds(f * L * step_rows, L * step_rows)], in_sem.at[f]) for f in range(F)]
    pairs = [(wind_hbm, wraw), (diff_hbm, draw), (b1_hbm, b1r), (b2_hbm, b2r), (b3_hbm, b3r), (w2_hbm, w2)]
    pairs += [(w1_hbm.at[f], w1.at[:, pl.ds(f * LEV, LEV)]) for f in range(F)]
    pairs += [(w3_hbm.at[f, pl.ds(own, L)], w3.at[pl.ds(f * L, L)]) for f in range(F)]
    loads += [pltpu.make_async_copy(s, d, in_sem.at[F + k]) for k, (s, d) in enumerate(pairs)]
    for copy in loads:
        copy.start()

    barrier = pltpu.get_barrier_semaphore()
    for d in ({"lon": east}, {"lon": west}, {"phys": other}):
        pl.semaphore_signal(barrier, inc=1, device_id=d, device_id_type=MESH)

    @pl.when(has_north)
    def _():
        pl.semaphore_signal(barrier, inc=1, device_id={"lat": north}, device_id_type=MESH)

    @pl.when(has_south)
    def _():
        pl.semaphore_signal(barrier, inc=1, device_id={"lat": south}, device_id_type=MESH)

    def lat_copy(rnd, side, f):
        return pltpu.make_async_remote_copy(
            src_ref=zs.at[rnd, side, f], dst_ref=zr.at[rnd, side, f],
            send_sem=zs_sem.at[rnd, side, f], recv_sem=zr_sem.at[rnd, side, f],
            device_id={"lat": south if side else north}, device_id_type=MESH)

    def lon_copy(m, side):
        return pltpu.make_async_remote_copy(
            src_ref=ls.at[m, side], dst_ref=lr.at[m, side],
            send_sem=ls_sem.at[m, side], recv_sem=lr_sem.at[m, side],
            device_id={"lon": west if side else east}, device_id_type=MESH)

    def x_copy(ph, f):
        rows = pl.ds(pl.multiple_of(f * LEV + phys * L, L), L)
        return pltpu.make_async_remote_copy(
            src_ref=xb.at[ph, :, rows], dst_ref=xb.at[ph, :, rows],
            send_sem=xs_sem.at[ph, f], recv_sem=xr_sem.at[ph, f],
            device_id={"phys": other}, device_id_type=MESH)

    can_send = (has_north, has_south)
    can_recv = (has_south, has_north)

    def lat_start(rnd, f):
        for side in range(2):
            @pl.when(can_send[side])
            def _():
                lat_copy(rnd, side, f).start()

    def lat_wait(rnd, f):
        for side in range(2):
            @pl.when(can_recv[side])
            def _():
                lat_copy(rnd, side, f).wait_recv()

    for side, there in enumerate(can_recv):
        @pl.when(jnp.logical_not(there))
        def _():
            zr[:, side] = jnp.zeros(zr.shape[:1] + zr.shape[2:], bf16)

    lane = lax.broadcasted_iota(jnp.int32, (BLK, LANES), 1)
    wide = lax.broadcasted_iota(jnp.int32, (BLK, C), 1)

    def blocks(body):
        def run(k, carry):
            body(pl.ds(pl.multiple_of(k * BLK, BLK), BLK), k * BLK)
            return carry
        lax.fori_loop(0, L // BLK, run, 0, unroll=True)

    def spaced(f, r, level, t):
        return pl.ds(((f * L + level) * tiles + t) * R + r, BLK, stride=step_rows)

    def natural(ref, f, r, level):
        return jnp.concatenate([ref[spaced(f, r, level, t), :] for t in range(tiles)], axis=1)

    def pack(q, rows, m):
        def body(lev, _):
            to_east = jnp.zeros((BLK, LANES), f32)
            to_west = jnp.zeros((BLK, LANES), f32)
            for f in range(F):
                for r in rows:
                    j = f * R + r
                    last = q[f, r, lev, C - LANES:]
                    first = q[f, r, lev, :LANES]
                    to_east = jnp.where(lane == j, jnp.broadcast_to(last[:, LANES - 1:], (BLK, LANES)), to_east)
                    to_west = jnp.where(lane == j, jnp.broadcast_to(first[:, :1], (BLK, LANES)), to_west)
            ls[m, 0, lev, :] = to_east.astype(bf16)
            ls[m, 1, lev, :] = to_west.astype(bf16)
        blocks(body)

    def lon_start(m):
        for side in range(2):
            lon_copy(m, side).start()

    def stencil(q, f, r, lev, rnd, m):
        j = f * R + r
        c = q[f, r, lev, :]
        hw = lr[m, 0, lev, :].astype(f32)[:, j:j + 1]
        he = lr[m, 1, lev, :].astype(f32)[:, j:j + 1]
        w = jnp.where(wide == 0, jnp.broadcast_to(hw, (BLK, C)), pltpu.roll(c, 1, 1))
        e = jnp.where(wide == C - 1, jnp.broadcast_to(he, (BLK, C)), pltpu.roll(c, C - 1, 1))
        s = q[f, r - 1, lev, :] if r else zr[rnd, 0, f, lev, :].astype(f32)
        n = q[f, r + 1, lev, :] if r < R - 1 else zr[rnd, 1, f, lev, :].astype(f32)
        return (cf[0, r, lev, :] * c + cf[1, r, lev, :] * e + cf[2, r, lev, :] * w
                + cf[3, r, lev, :] * n + cf[4, r, lev, :] * s)

    edge, inner = (0, R - 1), tuple(range(1, R - 1))
    phases = (inner, edge)

    for f in range(F):
        loads[f].wait()

        def body(lev, level):
            for r in range(R):
                v = natural(raw, f, r, level)
                q0[f, r, lev, :] = v
                if r == R - 1:
                    zs[0, 0, f, lev, :] = v.astype(bf16)
                if r == 0:
                    zs[0, 1, f, lev, :] = v.astype(bf16)
        blocks(body)

    pack(q0, range(R), 0)
    pl.semaphore_wait(barrier, 3 + has_north.astype(jnp.int32) + has_south.astype(jnp.int32))
    lon_start(0)
    for f in range(F):
        lat_start(0, f)

    for copy in loads[F:]:
        copy.wait()

    def coefficients(lev, level):
        for r in range(R):
            u = 0.5 * natural(wraw, 0, r, level)
            v = 0.5 * natural(wraw, 1, r, level)
            nu = natural(draw, 0, r, level)
            cf[0, r, lev, :] = 1.0 - 4.0 * nu
            cf[1, r, lev, :] = nu - u
            cf[2, r, lev, :] = nu + u
            cf[3, r, lev, :] = nu - v
            cf[4, r, lev, :] = nu + v
    blocks(coefficients)

    def columns(row):
        return jnp.transpose(jnp.broadcast_to(row, (LANES, LANES)))

    for k in range(H // LANES):
        b1[k * LANES:(k + 1) * LANES, :] = columns(b1r[k:k + 1, :])
        b2[k * LANES:(k + 1) * LANES, :] = columns(b2r[k:k + 1, :])
    for f in range(F):
        b3[f] = columns(b3r[f:f + 1, :])

    for side in range(2):
        lon_copy(0, side).wait_recv()

    def first_inner(lev, level):
        for r in inner:
            for f in range(F):
                q1[f, r, lev, :] = stencil(q0, f, r, lev, 0, 0)
    blocks(first_inner)
    pack(q1, inner, 1)
    lon_start(1)

    for f in range(F):
        lat_wait(0, f)

        def first_edge(lev, level):
            for side, r in ((1, 0), (0, R - 1)):
                v = stencil(q0, f, r, lev, 0, 0)
                q1[f, r, lev, :] = v
                zs[1, side, f, lev, :] = v.astype(bf16)
        blocks(first_edge)
        lat_start(1, f)
    pack(q1, edge, 2)
    lon_start(2)

    def second(f, ph, m):
        def body(lev, level):
            for i, r in enumerate(phases[ph]):
                v = stencil(q1, f, r, lev, 1, m)
                adv[ph, i, f, lev, :] = v
                xb[ph, i, pl.ds(pl.multiple_of(f * LEV + phys * L + level, BLK), BLK), :] = v.astype(bf16)
        blocks(body)
        x_copy(ph, f).start()

    def bias(ref):
        return jnp.concatenate([ref] * tiles, axis=1)

    def physics(ph):
        for i, r in enumerate(phases[ph]):
            pre = jnp.dot(w1[...], xb[ph, i], preferred_element_type=f32)
            act = silu(pre + bias(b1[...])).astype(bf16)
            pre = jnp.dot(w2[...], act, preferred_element_type=f32)
            act = silu(pre + bias(b2[...])).astype(bf16)
            for f in range(F):
                proj = jnp.dot(w3[f * L:(f + 1) * L, :], act, preferred_element_type=f32)
                ten = (proj + bias(b3[f, pl.ds(own, L), :])).astype(bf16).astype(f32)
                res = adv[ph, i, f] + ten
                for t in range(tiles):
                    oraw[pl.ds((f * L * tiles + t) * R + r, L, stride=step_rows), :] = (
                        res[:, t * LANES:(t + 1) * LANES])

    for side in range(2):
        lon_copy(1, side).wait_recv()
    for f in range(F):
        second(f, 0, 1)
    for f in range(F):
        x_copy(0, f).wait_recv()
    physics(0)

    for side in range(2):
        lon_copy(2, side).wait_recv()
    for f in range(F):
        lat_wait(1, f)
        second(f, 1, 2)
    for f in range(F):
        x_copy(1, f).wait_recv()
    physics(1)

    for f in range(F):
        for rnd in range(2):
            for side in range(2):
                @pl.when(can_send[side])
                def _():
                    lat_copy(rnd, side, f).wait_send()
            x_copy(rnd, f).wait_send()
    for m in range(3):
        for side in range(2):
            lon_copy(m, side).wait_send()


def as_stored(a, tiles):
    lead, rows = a.shape[:-2], a.shape[-2]
    a = a.reshape(lead + (rows, tiles, LANES))
    return jnp.swapaxes(a, -3, -2).reshape(-1, LANES)


def shards(tracers, wind_field, diffusivity, weight_in, bias_in, weight_mid, bias_mid, weight_out, bias_out):
    F, L, R, C = tracers.shape
    H, _, LEV = weight_in.shape
    tiles = C // LANES
    n = tracers.size // LANES
    dma = pltpu.SemaphoreType.DMA
    V = pltpu.VMEM
    out = pl.pallas_call(
        functools.partial(kernel, (F, L, R, C, H, LEV)),
        out_shape=jax.ShapeDtypeStruct((n, LANES), f32),
        in_specs=[pl.BlockSpec(memory_space=pltpu.HBM)] * 9,
        out_specs=pl.BlockSpec(memory_space=pltpu.VMEM),
        scratch_shapes=[
            V((n, LANES), f32), V((2 * n // F, LANES), f32), V((n // F, LANES), f32),
            V((H, F * LEV), bf16), V((H, H), bf16), V((F * L, H), bf16),
            V((H // LANES, LANES), f32), V((H // LANES, LANES), f32), V((F, LEV), f32),
            V((H, LANES), f32), V((H, LANES), f32), V((F, LEV, LANES), f32),
            V((F, R, L, C), f32), V((F, R, L, C), f32), V((2, 2, F, L, C), f32), V((5, R, L, C), f32),
            V((2, 2, F, L, C), bf16), V((2, 2, F, L, C), bf16),
            V((3, 2, L, LANES), bf16), V((3, 2, L, LANES), bf16),
            V((2, 2, F * LEV, C), bf16),
            dma((3 * F + 6,)), dma((2, 2, F)), dma((2, 2, F)), dma((3, 2)), dma((3, 2)),
            dma((2, F)), dma((2, F)),
        ],
        compiler_params=pltpu.CompilerParams(
            collective_id=0, has_side_effects=True, vmem_limit_bytes=32 * 2**20),
    )(*(pltpu.with_memory_space_constraint(a, pltpu.HBM) for a in (
        as_stored(tracers, tiles), as_stored(wind_field, tiles), as_stored(diffusivity, tiles),
        jnp.swapaxes(weight_in, 0, 1), bias_in.reshape(-1, LANES), weight_mid,
        bias_mid.reshape(-1, LANES), weight_out, bias_out,
    )))
    out = out.reshape(F, L, tiles, R, LANES)
    return jnp.swapaxes(out, 2, 3).reshape(F, L, R, C)


def solution(mesh):
    placed = (
        P(None, "phys", "lat", "lon"), P(None, "phys", "lat", "lon"), P("phys", "lat", "lon"),
        P(), P(), P(), P(), P(), P(),
    )
    return jax.shard_map(
        shards, mesh=mesh, in_specs=placed, out_specs=P(None, "phys", "lat", "lon"), check_vma=False
    )
```
